256 devices in a mesh: grp: 16 (over x, y_hi, core), dev: 16 (over z, y_lo).
Axes of the slice: x: 4, y: 4 (y_hi: 2, y_lo: 2; y = y_hi * 2 + y_lo), z: 8, core: 2. Of those that a mesh axis runs over, the one named last changes fastest.
Arguments:
- queries: bfloat16 [1024, 8192], P(('grp', 'dev')), may hold values from -10 to 10
- root_keys: bfloat16 [32768, 1024], P(('grp', 'dev')), may hold values from -4 to 4
- root_values: bfloat16 [32768, 1024], P(('grp', 'dev')), may hold values from -12 to 12
- prefix_keys: bfloat16 [16, 16, 8, 64, 1024], P('grp', 'dev'), may hold values from -6 to 6
- prefix_values: bfloat16 [16, 16, 8, 64, 1024], P('grp', 'dev'), may hold values from -12 to 12
- page_table: int32 [4, 16, 4], P(None, 'dev'), may hold values from 0 to 7, as said below
- task_ids: int32 [16], P('grp'), may hold values from 0 to 3
- suffix_keys: bfloat16 [1024, 128, 1024], P(('grp', 'dev')), may hold values from -6.375 to 6.375
- suffix_values: bfloat16 [1024, 128, 1024], P(('grp', 'dev')), may hold values from -12 to 12
- suffix_lengths: int32 [1024], P(('grp', 'dev')), may hold values from 1 to 128, as said below
Outputs:
- attended: bfloat16 [1024, 8192], P(('grp', 'dev'))
The draws below stay inside these ranges and needn't reach their ends.
Inputs may be any that keep to these rules, and one draw needn't show every extreme that they name: `page_table`: entries of one task and one member name distinct pages of that member's pool. `suffix_lengths`: every device holds a row with all 128 slots live.
All inputs are finite; a program needn't handle non-finite values.
Results may differ from the reference program's by a relative error of at most 0.013.
Values may be sent and summed in bfloat16 or wider, within the bound.
No kernel may reach another device: no remote copies, remote signals or barrier semaphores. Data moves between devices by JAX's collectives and lax.ppermute only.
A program may use at most 64 MiB of HBM per device.

```python
import jax
import jax.numpy as jnp
from jax import lax

HD = 128
KVH = 8
QPK = 8
ROW_DEV = 4
PPD = 4
PAGE = 64
SUF = 128
TASKS = 4
POOL_DEV = 8
GROUPS = 16
MEMBERS = 16
ROWS = 1024
ROOT = 32768


def draw_queries(key, part):
    key = jax.random.fold_in(key, 11)
    values_drawn = 2.5 * jax.random.truncated_normal(key, -4.0, 4.0, (ROWS, KVH, QPK, HD), jnp.float32)
    return values_drawn.reshape(ROWS, KVH * QPK * HD).astype(jnp.bfloat16)


def draw_root_keys(key, part):
    key = jax.random.fold_in(key, 12)
    values_drawn = jax.random.truncated_normal(key, -4.0, 4.0, (ROOT, KVH * HD), jnp.float32)
    return values_drawn.astype(jnp.bfloat16)


def draw_page_table(key, part):
    key = jax.random.fold_in(key, 13)
    key_list = jax.random.split(key, TASKS * MEMBERS)

    def one_table(single_key):
        return jax.random.permutation(single_key, POOL_DEV)[:PPD]
    chosen = jax.vmap(one_table)(key_list)
    return chosen.reshape(TASKS, MEMBERS, PPD).astype(jnp.int32)


def draw_suffix_lengths(key, part):
    key = jax.random.fold_in(key, 14)
    earlier = jax.random.randint(jax.random.fold_in(key, 1), (ROWS,), 1, SUF + 1)
    later = jax.random.randint(jax.random.fold_in(key, 2), (ROWS,), 1, SUF + 1)
    lengths_drawn = jnp.minimum(earlier, later)
    picked = jax.random.randint(jax.random.fold_in(key, 3), (ROWS // ROW_DEV,), 0, ROW_DEV)
    filled = jnp.arange(ROWS) % ROW_DEV == jnp.repeat(picked, ROW_DEV)
    return jnp.where(filled, SUF, lengths_drawn).astype(jnp.int32)


def with_ends(entries, key, smallest, top_value):
    place = [jax.random.randint(jax.random.fold_in(key, axis), (), 0, length) for axis, length in enumerate(entries.shape)]
    longest = entries.shape.index(max(entries.shape))
    beside = place[:longest] + [(place[longest] + 1) % entries.shape[longest]] + place[longest + 1:]
    return entries.at[tuple(place)].set(smallest).at[tuple(beside)].set(top_value)


def shard_levels(own_key, shape, pieces, low, largest):
    level, own = 1.0, jax.random.fold_in(own_key, 6)
    for position, shards_of in pieces:
        draws = jnp.exp(jax.random.uniform(jax.random.fold_in(own, position), (shards_of,), jnp.float32, low / len(pieces), largest / len(pieces)))
        level = level * jnp.repeat(draws, shape[position] // shards_of).reshape([-1 if axis == position else 1 for axis in range(len(shape))])
    return level


def scatter_about(own_key, shape, scale, bound, cuts=(), held_as=jnp.bfloat16):
    values = scale * jax.random.normal(own_key, shape, jnp.float32)
    if cuts:
        values = values * shard_levels(own_key, shape, cuts, -0.22, 0.18)
    return jnp.clip(values, -bound, bound).astype(held_as)


def setup_inputs(seed: int = 0) -> dict:
    arg_keys = jax.random.split(jax.random.key(seed), 11)
    return {
        "queries": draw_queries(jax.random.fold_in(arg_keys[10], 71), 0),
        "root_keys": draw_root_keys(jax.random.fold_in(arg_keys[10], 71), 0),
        "root_values": scatter_about(arg_keys[2], (ROOT, KVH * HD), 2.0, 12.0, ((0, 256),)),
        "prefix_keys": scatter_about(arg_keys[3], (GROUPS, MEMBERS, POOL_DEV, PAGE, KVH * HD), 1.0, 6.0, ((0, 16), (1, 16))),
        "prefix_values": scatter_about(arg_keys[4], (GROUPS, MEMBERS, POOL_DEV, PAGE, KVH * HD), 2.0, 12.0, ((0, 16), (1, 16))),
        "page_table": draw_page_table(jax.random.fold_in(arg_keys[10], 71), 0),
        "task_ids": with_ends(jax.random.randint(arg_keys[6], (GROUPS,), 0, TASKS), jax.random.fold_in(arg_keys[6], 1), 0, TASKS - 1).astype(jnp.int32),
        "suffix_keys": scatter_about(arg_keys[7], (ROWS, SUF, KVH * HD), 1.6, 6.375, ((0, 256),)),
        "suffix_values": scatter_about(arg_keys[8], (ROWS, SUF, KVH * HD), 2.0, 12.0, ((0, 256),)),
        "suffix_lengths": draw_suffix_lengths(jax.random.fold_in(arg_keys[10], 71), 0),
    }


def reference(queries, root_keys, root_values, prefix_keys, prefix_values, page_table, task_ids, suffix_keys, suffix_values, suffix_lengths):
    softmax_scale = HD ** -0.5
    group_rows = ROW_DEV * MEMBERS
    root_key_heads = root_keys.astype(jnp.float32).reshape(ROOT, KVH, HD)
    root_value_heads = root_values.astype(jnp.float32).reshape(ROOT, KVH, HD)

    def pick_pages(pool_rows, page_rows):
        return pool_rows[page_rows]

    def one_group(group_index):
        row_start = group_index * group_rows
        query_heads = lax.dynamic_slice_in_dim(queries, row_start, group_rows, 0).astype(jnp.float32).reshape(group_rows, KVH, QPK, HD)
        page_rows = page_table[task_ids[group_index]]
        prefix_key_rows = jax.vmap(pick_pages)(prefix_keys[group_index], page_rows).astype(jnp.float32).reshape(-1, KVH, HD)
        prefix_value_rows = jax.vmap(pick_pages)(prefix_values[group_index], page_rows).astype(jnp.float32).reshape(-1, KVH, HD)
        shared_keys = jnp.concatenate([root_key_heads, prefix_key_rows], axis=0)
        shared_values = jnp.concatenate([root_value_heads, prefix_value_rows], axis=0)
        own_suffix_keys = lax.dynamic_slice_in_dim(suffix_keys, row_start, group_rows, 0).astype(jnp.float32).reshape(group_rows, SUF, KVH, HD)
        own_suffix_values = lax.dynamic_slice_in_dim(suffix_values, row_start, group_rows, 0).astype(jnp.float32).reshape(group_rows, SUF, KVH, HD)
        own_lengths = lax.dynamic_slice_in_dim(suffix_lengths, row_start, group_rows, 0)
        shared_scores = jnp.einsum("rkgd,tkd->rkgt", query_heads, shared_keys) * softmax_scale
        suffix_scores = jnp.einsum("rkgd,rskd->rkgs", query_heads, own_suffix_keys) * softmax_scale
        live_slots = (jnp.arange(SUF, dtype=jnp.int32)[None, :] < own_lengths[:, None])[:, None, None, :]
        suffix_scores = jnp.where(live_slots, suffix_scores, -1e30)
        peaks = jnp.maximum(jnp.max(shared_scores, axis=-1), jnp.max(suffix_scores, axis=-1))
        shared_weights = jnp.exp(shared_scores - peaks[..., None])
        suffix_weights = jnp.where(live_slots, jnp.exp(suffix_scores - peaks[..., None]), 0.0)
        totals = jnp.sum(shared_weights, axis=-1) + jnp.sum(suffix_weights, axis=-1)
        shared_rounded = lax.optimization_barrier(shared_weights.astype(jnp.bfloat16)).astype(jnp.float32)
        suffix_rounded = lax.optimization_barrier(suffix_weights.astype(jnp.bfloat16)).astype(jnp.float32)
        weighted = jnp.einsum("rkgt,tkd->rkgd", shared_rounded, shared_values)
        weighted = weighted + jnp.einsum("rkgs,rskd->rkgd", suffix_rounded, own_suffix_values)
        result = weighted / totals[..., None]
        return result.astype(jnp.bfloat16).reshape(group_rows, KVH * QPK * HD)

    outputs = lax.map(one_group, jnp.arange(GROUPS, dtype=jnp.int32))
    return outputs.reshape(ROWS, KVH * QPK * HD)
```

```python
import functools

import jax
import jax.numpy as jnp
from jax import lax
from jax.experimental import pallas as pl
from jax.experimental.pallas import tpu as pltpu
from jax.sharding import PartitionSpec as P

HD = 128
KVH = 8
QPK = 8
MEMBERS = 16
OWN = 4
UNIT = OWN * QPK
SUF = 128
PPD = 4
PAGE = 64
SCALE = HD ** (-0.5)
LOG2E = 1.4426950408889634
VMEM_LIMIT = 40 * 1024 * 1024
O_CHUNKS = ((0, 4), (4, 4))


def grp_index(x, y_hi, core):
    return (x % 4) * 4 + (y_hi % 2) * 2 + core


def grp_pairs(target):
    return [
        (grp_index(x, y, c), grp_index(*target(x, y, c)))
        for x in range(4)
        for y in range(2)
        for c in range(2)
    ]


def to_other_core(array):
    return lax.ppermute(array, "grp", grp_pairs(lambda x, y, c: (x, y, 1 - c)))


def along_y(array):
    return lax.ppermute(array, "grp", grp_pairs(lambda x, y, c: (x, 1 - y, c)))


def along_x(array):
    return lax.ppermute(array, "grp", grp_pairs(lambda x, y, c: (x + 1 - 2 * c, y, c)))


def gather_root(own):
    other = to_other_core(own)
    near = along_x(own)
    across = along_y(own)
    near_other = along_x(other)
    far = along_x(near)
    across_near = along_y(near)
    across_other = to_other_core(across)
    across_near_other = along_x(across_other)
    across_far = along_x(across_near)
    received = [near, near_other, far, across_near, across_near_other, across_far]
    return [own, other, across, across_other] + received + [to_other_core(r) for r in received]


def nt_dot(a, b):
    return lax.dot_general(a, b, (((1,), (1,)), ((), ())), preferred_element_type=jnp.float32)


def split_three(value):
    first = value.astype(jnp.bfloat16)
    rest = value - first.astype(jnp.float32)
    second = rest.astype(jnp.bfloat16)
    third = (rest - second.astype(jnp.float32)).astype(jnp.bfloat16)
    return first, second, third


def attention_kernel(head_start, heads, pieces, *refs):
    task_ref, table_ref, q_ref = refs[:3]
    piece_refs = refs[3 : 3 + pieces]
    pool_k, pool_v, out_ref = refs[3 + pieces : 6 + pieces]
    page_k, page_v, stats_ref, sems = refs[6 + pieces :]
    task = task_ref[0]
    copies = []
    for j in range(PPD):
        page = table_ref[task, j]
        rows = pl.ds(j * PAGE, PAGE)
        copies.append(pltpu.make_async_copy(pool_k.at[page], page_k.at[rows], sems.at[j]))
        copies.append(pltpu.make_async_copy(pool_v.at[page], page_v.at[rows], sems.at[PPD + j]))
    for copy in copies:
        copy.start()
    stats_ref[...] = jnp.zeros_like(stats_ref)
    for copy in copies:
        copy.wait()
    rows_all = MEMBERS * UNIT

    def one_head(index, carry):
        lanes = pl.ds(pl.multiple_of((head_start + index) * HD, HD), HD)
        q = q_ref[:, head_start + index].reshape(rows_all, HD)
        keys = jnp.concatenate([r[0, :, lanes] for r in piece_refs] + [page_k[:, lanes]], axis=0)
        scores = nt_dot(q, keys)
        peaks = jnp.max(scores, axis=1, keepdims=True)
        weights = jnp.exp2((scores - peaks) * (SCALE * LOG2E))
        totals = jnp.sum(weights, axis=1, keepdims=True)
        values = jnp.concatenate([r[1, :, lanes] for r in piece_refs] + [page_v[:, lanes]], axis=0)
        weighted = jnp.dot(weights.astype(jnp.bfloat16), values, preferred_element_type=jnp.float32)
        out_ref[:, pl.ds(index, 1)] = (
            (weighted / totals).astype(jnp.bfloat16).reshape(MEMBERS, 1, UNIT, HD)
        )
        lse = peaks * SCALE + jnp.log(totals)
        lane = lax.broadcasted_iota(jnp.int32, (rows_all, HD), 1)
        stats_ref[...] = jnp.where(lane == index, lse, stats_ref[...])
        return carry

    lax.fori_loop(0, heads, one_head, 0)
    lane = lax.broadcasted_iota(jnp.int32, (rows_all, HD), 1)
    first, second, third = split_three(stats_ref[...])
    packed = (
        first.astype(jnp.float32)
        + pltpu.roll(second.astype(jnp.float32), KVH, 1)
        + pltpu.roll(third.astype(jnp.float32), 2 * KVH, 1)
    )
    packed = jnp.where(lane < 3 * KVH, packed, 0.0)
    out_ref[:, heads] = packed.astype(jnp.bfloat16).reshape(MEMBERS, UNIT, HD)


def attend(head_start, heads, task, table, q_all, pieces, pool_k, pool_v):
    rows_all = MEMBERS * UNIT
    keys = 128 * len(pieces) + PPD * PAGE
    vmem = pl.BlockSpec(memory_space=pltpu.VMEM)
    smem = pl.BlockSpec(memory_space=pltpu.SMEM)
    hbm = pl.BlockSpec(memory_space=pl.ANY)
    return pl.pallas_call(
        functools.partial(attention_kernel, head_start, heads, len(pieces)),
        out_shape=jax.ShapeDtypeStruct((MEMBERS, heads + 1, UNIT, HD), jnp.bfloat16),
        in_specs=[smem, smem, vmem] + [vmem] * len(pieces) + [hbm, hbm],
        out_specs=vmem,
        scratch_shapes=[
            pltpu.VMEM((PPD * PAGE, KVH * HD), jnp.bfloat16),
            pltpu.VMEM((PPD * PAGE, KVH * HD), jnp.bfloat16),
            pltpu.VMEM((rows_all, HD), jnp.float32),
            pltpu.SemaphoreType.DMA((2 * PPD,)),
        ],
        compiler_params=pltpu.CompilerParams(vmem_limit_bytes=VMEM_LIMIT),
        cost_estimate=pl.CostEstimate(
            flops=4 * heads * rows_all * keys * HD,
            bytes_accessed=4 * keys * heads * HD,
            transcendentals=heads * rows_all * keys,
        ),
        name="attend",
    )(task, table, q_all, *pieces, pool_k, pool_v)


def suffix_kernel(length_ref, q_ref, k_ref, v_ref, out_ref, lse_ref):
    slots = OWN * SUF
    row = lax.broadcasted_iota(jnp.int32, (UNIT, slots), 0) // QPK
    slot = lax.broadcasted_iota(jnp.int32, (UNIT, slots), 1)
    live = jnp.zeros((UNIT, slots), jnp.bool_)
    for i in range(OWN):
        low = i * SUF
        live = live | ((row == i) & (slot >= low) & (slot < low + length_ref[i]))
    for k in range(KVH):
        lanes = slice(k * HD, (k + 1) * HD)
        keys = jnp.concatenate([k_ref[i, :, lanes] for i in range(OWN)], axis=0)
        values = jnp.concatenate([v_ref[i, :, lanes] for i in range(OWN)], axis=0)
        scores = jnp.where(live, nt_dot(q_ref[k], keys) * SCALE, -1e30)
        peaks = jnp.max(scores, axis=1, keepdims=True)
        weights = jnp.where(live, jnp.exp(scores - peaks), 0.0)
        totals = jnp.sum(weights, axis=1, keepdims=True)
        weighted = jnp.dot(weights.astype(jnp.bfloat16), values, preferred_element_type=jnp.float32)
        out_ref[k] = weighted / totals
        lse_ref[k] = jnp.broadcast_to(peaks + jnp.log(totals), (UNIT, HD))


def attend_suffix(lengths, q_units, suffix_keys, suffix_values):
    vmem = pl.BlockSpec(memory_space=pltpu.VMEM)
    shape = jax.ShapeDtypeStruct((KVH, UNIT, HD), jnp.float32)
    return pl.pallas_call(
        suffix_kernel,
        out_shape=(shape, shape),
        in_specs=[pl.BlockSpec(memory_space=pltpu.SMEM), vmem, vmem, vmem],
        out_specs=(vmem, vmem),
        compiler_params=pltpu.CompilerParams(vmem_limit_bytes=VMEM_LIMIT),
        cost_estimate=pl.CostEstimate(
            flops=4 * KVH * UNIT * OWN * SUF * HD, bytes_accessed=2 << 20, transcendentals=KVH * UNIT * OWN * SUF
        ),
        name="attend_suffix",
    )(lengths, q_units, suffix_keys, suffix_values)


def merge_kernel(head_start, heads, parts_ref, out_suf_ref, lse_suf_ref, out_ref):
    stats = parts_ref[:, heads].astype(jnp.float32).reshape(MEMBERS * UNIT, HD)
    lse = stats + pltpu.roll(stats, HD - KVH, 1) + pltpu.roll(stats, HD - 2 * KVH, 1)
    for k in range(heads):
        own_lse = lse_suf_ref[head_start + k]
        column = jnp.broadcast_to(lse[:, k : k + 1], (MEMBERS * UNIT, HD)).reshape(MEMBERS, UNIT, HD)
        top = jnp.maximum(jnp.max(column, axis=0), own_lse)
        factor = jnp.exp(column - top[None])
        own_factor = jnp.exp(own_lse - top)
        weighted = jnp.sum(parts_ref[:, k].astype(jnp.float32) * factor, axis=0)
        weighted = weighted + out_suf_ref[head_start + k] * own_factor
        totals = jnp.sum(factor, axis=0) + own_factor
        out_ref[k] = (weighted / totals).astype(jnp.bfloat16)


def merge(head_start, heads, parts, out_suf, lse_suf):
    vmem = pl.BlockSpec(memory_space=pltpu.VMEM)
    return pl.pallas_call(
        functools.partial(merge_kernel, head_start, heads),
        out_shape=jax.ShapeDtypeStruct((heads, UNIT, HD), jnp.bfloat16),
        in_specs=[vmem] * 3,
        out_specs=vmem,
        compiler_params=pltpu.CompilerParams(vmem_limit_bytes=VMEM_LIMIT),
        cost_estimate=pl.CostEstimate(
            flops=4 * MEMBERS * heads * UNIT * HD, bytes_accessed=2 * MEMBERS * heads * UNIT * HD, transcendentals=0
        ),
        name="merge",
    )(parts, out_suf, lse_suf)


def per_device(
    queries,
    root_keys,
    root_values,
    prefix_keys,
    prefix_values,
    page_table,
    task_ids,
    suffix_keys,
    suffix_values,
    suffix_lengths,
):
    q_units = queries.reshape(OWN, KVH, QPK, HD).transpose(1, 0, 2, 3).reshape(KVH, UNIT, HD)
    pieces = gather_root(jnp.stack((root_keys, root_values)))
    q_tiled = jnp.broadcast_to(q_units[None], (MEMBERS, KVH, UNIT, HD))
    q_all = lax.all_to_all(q_tiled, "dev", 0, 0)
    out_suf, lse_suf = attend_suffix(suffix_lengths, q_units, suffix_keys, suffix_values)
    outs = []
    for head_start, heads in O_CHUNKS:
        part = attend(
            head_start, heads, task_ids, page_table[:, 0], q_all, pieces, prefix_keys[0, 0], prefix_values[0, 0]
        )
        parts = lax.all_to_all(part, "dev", 0, 0)
        outs.append(merge(head_start, heads, parts, out_suf, lse_suf))
    merged = jnp.concatenate(outs, axis=0)
    return merged.reshape(KVH, OWN, QPK, HD).transpose(1, 0, 2, 3).reshape(OWN, KVH * QPK * HD)


def solution(mesh):
    placed = (
        P(("grp", "dev"), None),
        P(("grp", "dev"), None),
        P(("grp", "dev"), None),
        P("grp", "dev", None, None, None),
        P("grp", "dev", None, None, None),
        P(None, "dev", None),
        P("grp"),
        P(("grp", "dev"), None, None),
        P(("grp", "dev"), None, None),
        P(("grp", "dev")),
    )
    return jax.shard_map(
        per_device, mesh=mesh, in_specs=placed, out_specs=P(("grp", "dev"), None), check_vma=False
    )
```

```python
import functools

import jax
import jax.numpy as jnp
from jax import lax
from jax.experimental import pallas as pl
from jax.experimental.pallas import tpu as pltpu
from jax.sharding import PartitionSpec as P

HD = 128
KVH = 8
QPK = 8
MEMBERS = 16
OWN = 4
UNIT = OWN * QPK
SUF = 128
PPD = 4
PAGE = 64
SCALE = HD ** (-0.5)
LOG2E = 1.4426950408889634
ROWS_ALL = MEMBERS * UNIT
VMEM_LIMIT = 16 * 1024 * 1024
ATTEND_VMEM = 60 * 1024 * 1024
PARTS = 2
STEPS = 3


def grp_index(x, y_hi, core):
    return (x % 4) * 4 + (y_hi % 2) * 2 + core


def grp_pairs(target):
    return [
        (grp_index(x, y, c), grp_index(*target(x, y, c)))
        for x in range(4)
        for y in range(2)
        for c in range(2)
    ]


def to_other_core(array):
    return lax.ppermute(array, "grp", grp_pairs(lambda x, y, c: (x, y, 1 - c)))


def along_y(array):
    return lax.ppermute(array, "grp", grp_pairs(lambda x, y, c: (x, 1 - y, c)))


def along_x(array):
    return lax.ppermute(array, "grp", grp_pairs(lambda x, y, c: (x + 1 - 2 * c, y, c)))


def after(array, *others):
    return lax.optimization_barrier((array, *others))[0]


def gather_root(own):
    other = to_other_core(own)
    near = along_x(own)
    across = along_y(own)
    near_other = along_x(other)
    far = along_x(near)
    across = after(across, near_other)
    across_near = along_x(across)
    across_other = to_other_core(across)
    across_near_other = along_x(across_other)
    across_far = along_x(across_near)
    received = [near, near_other, far, across_near, across_near_other, across_far]
    return [own, other, across, across_other] + received + [to_other_core(r) for r in received]


def nt_dot(a, b):
    return lax.dot_general(a, b, (((1,), (1,)), ((), ())), preferred_element_type=jnp.float32)


def split_three(value):
    first = value.astype(jnp.bfloat16)
    rest = value - first.astype(jnp.float32)
    second = rest.astype(jnp.bfloat16)
    third = (rest - second.astype(jnp.float32)).astype(jnp.bfloat16)
    return first, second, third


def flash_step(q, keys, values, state):
    scores = nt_dot(q, keys)
    peaks = jnp.max(scores, axis=1, keepdims=True)
    if state is not None:
        peaks = jnp.maximum(peaks, state[0])
    weights = jnp.exp2((scores - peaks) * (SCALE * LOG2E)).astype(jnp.bfloat16)
    widened = jnp.concatenate([values, jnp.ones_like(values)], axis=1)
    both = jnp.dot(weights, widened, preferred_element_type=jnp.float32)
    weighted, totals = both[:, :HD], both[:, HD:]
    if state is not None:
        factor = jnp.exp2((state[0] - peaks) * (SCALE * LOG2E))
        totals = totals + state[1] * factor
        weighted = weighted + state[2] * factor
    return peaks, totals, weighted


def attention_kernel(pieces, *refs):
    task_ref, table_ref, q_ref = refs[:3]
    piece_refs = refs[3 : 3 + pieces]
    pool_k, pool_v, out_ref, held_ref, stats_ref, sems = refs[3 + pieces :]
    task = task_ref[0]
    root_rows = 128 * pieces
    copies = []
    for part in range(PARTS):
        lanes = pl.ds(part * (KVH * HD // PARTS), KVH * HD // PARTS)
        group = []
        for i, piece in enumerate(piece_refs):
            target = held_ref.at[:, pl.ds(i * 128, 128), lanes]
            group.append(pltpu.make_async_copy(piece.at[:, :, lanes], target, sems.at[part, i]))
        for j in range(PPD):
            page = table_ref[task, j]
            rows = pl.ds(root_rows + j * PAGE, PAGE)
            for side, pool in enumerate((pool_k, pool_v)):
                target = held_ref.at[side, rows, lanes]
                sem = sems.at[part, pieces + 2 * j + side]
                group.append(pltpu.make_async_copy(pool.at[page, :, lanes], target, sem))
        copies.append(group)
    for group in copies:
        for copy in group:
            copy.start()
    stats_ref[...] = jnp.zeros_like(stats_ref)
    size = (root_rows + PPD * PAGE) // STEPS

    def one_head(k, carry):
        lanes = pl.ds(pl.multiple_of(k * HD, HD), HD)
        q = q_ref[:, k].reshape(ROWS_ALL, HD)
        state = None
        for i in range(STEPS):
            rows = slice(i * size, (i + 1) * size)
            state = flash_step(q, held_ref[0, rows, lanes], held_ref[1, rows, lanes], state)
        peaks, totals, weighted = state
        rows = pl.ds(pl.multiple_of(k * UNIT, UNIT), UNIT)
        out_ref[:, rows] = (weighted / totals).astype(jnp.bfloat16).reshape(MEMBERS, UNIT, HD)
        lse = peaks * SCALE + jnp.log(totals)
        lane = lax.broadcasted_iota(jnp.int32, (ROWS_ALL, HD), 1)
        stats_ref[...] = jnp.where(lane == k, lse, stats_ref[...])
        return carry

    for part, group in enumerate(copies):
        for copy in group:
            copy.wait()
        lax.fori_loop(part * (KVH // PARTS), (part + 1) * (KVH // PARTS), one_head, 0)
    first, second, third = split_three(stats_ref[...])
    packed = (
        first.astype(jnp.float32)
        + pltpu.roll(second.astype(jnp.float32), KVH, 1)
        + pltpu.roll(third.astype(jnp.float32), 2 * KVH, 1)
    )
    packed = packed.reshape(MEMBERS, 2, UNIT // 2, HD)
    upper = pltpu.roll(packed[:, 1].reshape(ROWS_ALL // 2, HD), HD // 2, 1)
    packed = packed[:, 0].reshape(ROWS_ALL // 2, HD) + upper
    out_ref[:, KVH * UNIT :] = packed.astype(jnp.bfloat16).reshape(MEMBERS, UNIT // 2, HD)


def attend(task, table, q_all, pieces, pool_k, pool_v):
    keys = 128 * len(pieces) + PPD * PAGE
    vmem = pl.BlockSpec(memory_space=pltpu.VMEM)
    smem = pl.BlockSpec(memory_space=pltpu.SMEM)
    hbm = pl.BlockSpec(memory_space=pl.ANY)
    return pl.pallas_call(
        functools.partial(attention_kernel, len(pieces)),
        out_shape=jax.ShapeDtypeStruct((MEMBERS, KVH * UNIT + UNIT // 2, HD), jnp.bfloat16),
        in_specs=[smem, smem, vmem] + [hbm] * len(pieces) + [hbm, hbm],
        out_specs=vmem,
        scratch_shapes=[
            pltpu.VMEM((2, keys, KVH * HD), jnp.bfloat16),
            pltpu.VMEM((ROWS_ALL, HD), jnp.float32),
            pltpu.SemaphoreType.DMA((PARTS, len(pieces) + 2 * PPD)),
        ],
        compiler_params=pltpu.CompilerParams(vmem_limit_bytes=ATTEND_VMEM),
        cost_estimate=attend_cost(keys),
        name="attend",
    )(task, table, q_all, *pieces, pool_k, pool_v)


def attend_cost(keys):
    return pl.CostEstimate(
        flops=8 * KVH * ROWS_ALL * keys * HD,
        bytes_accessed=4 * keys * KVH * HD,
        transcendentals=KVH * ROWS_ALL * keys,
    )


def suffix_kernel(length_ref, q_ref, k_ref, v_ref, out_ref, lse_ref):
    slots = OWN * SUF
    row = lax.broadcasted_iota(jnp.int32, (UNIT, slots), 0) // QPK
    slot = lax.broadcasted_iota(jnp.int32, (UNIT, slots), 1)
    live = jnp.zeros((UNIT, slots), jnp.bool_)
    for i in range(OWN):
        low = i * SUF
        live = live | ((row == i) & (slot >= low) & (slot < low + length_ref[i]))
    for k in range(KVH):
        lanes = slice(k * HD, (k + 1) * HD)
        keys = jnp.concatenate([k_ref[i, :, lanes] for i in range(OWN)], axis=0)
        values = jnp.concatenate([v_ref[i, :, lanes] for i in range(OWN)], axis=0)
        scores = jnp.where(live, nt_dot(q_ref[k], keys) * SCALE, -1e30)
        peaks = jnp.max(scores, axis=1, keepdims=True)
        weights = jnp.where(live, jnp.exp(scores - peaks), 0.0)
        totals = jnp.sum(weights, axis=1, keepdims=True)
        weighted = jnp.dot(weights.astype(jnp.bfloat16), values, preferred_element_type=jnp.float32)
        out_ref[k] = weighted / totals
        lse_ref[k] = jnp.broadcast_to(peaks + jnp.log(totals), (UNIT, HD))


def attend_suffix(lengths, q_units, suffix_keys, suffix_values):
    vmem = pl.BlockSpec(memory_space=pltpu.VMEM)
    shape = jax.ShapeDtypeStruct((KVH, UNIT, HD), jnp.float32)
    return pl.pallas_call(
        suffix_kernel,
        out_shape=(shape, shape),
        in_specs=[pl.BlockSpec(memory_space=pltpu.SMEM), vmem, vmem, vmem],
        out_specs=(vmem, vmem),
        compiler_params=pltpu.CompilerParams(vmem_limit_bytes=VMEM_LIMIT),
        cost_estimate=pl.CostEstimate(
            flops=4 * KVH * UNIT * OWN * SUF * HD, bytes_accessed=2 << 20, transcendentals=KVH * UNIT * OWN * SUF
        ),
        name="attend_suffix",
    )(lengths, q_units, suffix_keys, suffix_values)


def merge_kernel(parts_ref, out_suf_ref, lse_suf_ref, out_ref):
    stats = parts_ref[:, KVH * UNIT :].astype(jnp.float32)
    upper = pltpu.roll(stats.reshape(ROWS_ALL // 2, HD), HD // 2, 1).reshape(MEMBERS, UNIT // 2, HD)
    stats = jnp.concatenate([stats, upper], axis=1).reshape(ROWS_ALL, HD)
    lse = stats + pltpu.roll(stats, HD - KVH, 1) + pltpu.roll(stats, HD - 2 * KVH, 1)
    for k in range(KVH):
        own_lse = lse_suf_ref[k]
        column = jnp.broadcast_to(lse[:, k : k + 1], (ROWS_ALL, HD)).reshape(MEMBERS, UNIT, HD)
        top = jnp.maximum(jnp.max(column, axis=0), own_lse)
        factor = jnp.exp(column - top[None])
        own_factor = jnp.exp(own_lse - top)
        part = parts_ref[:, k * UNIT : (k + 1) * UNIT].astype(jnp.float32)
        weighted = jnp.sum(part * factor, axis=0) + out_suf_ref[k] * own_factor
        totals = jnp.sum(factor, axis=0) + own_factor
        out_ref[k] = (weighted / totals).astype(jnp.bfloat16)


def merge(parts, out_suf, lse_suf):
    vmem = pl.BlockSpec(memory_space=pltpu.VMEM)
    return pl.pallas_call(
        merge_kernel,
        out_shape=jax.ShapeDtypeStruct((KVH, UNIT, HD), jnp.bfloat16),
        in_specs=[vmem] * 3,
        out_specs=vmem,
        compiler_params=pltpu.CompilerParams(vmem_limit_bytes=VMEM_LIMIT),
        cost_estimate=pl.CostEstimate(
            flops=4 * KVH * ROWS_ALL * HD, bytes_accessed=2 * KVH * ROWS_ALL * HD, transcendentals=0
        ),
        name="merge",
    )(parts, out_suf, lse_suf)


def per_device(
    queries,
    root_keys,
    root_values,
    prefix_keys,
    prefix_values,
    page_table,
    task_ids,
    suffix_keys,
    suffix_values,
    suffix_lengths,
):
    q_units = queries.reshape(OWN, KVH, QPK, HD).transpose(1, 0, 2, 3).reshape(KVH, UNIT, HD)
    pieces = gather_root(jnp.stack((root_keys, root_values)))
    q_tiled = jnp.broadcast_to(q_units[None], (MEMBERS, KVH, UNIT, HD))
    q_all = lax.all_to_all(q_tiled, "dev", 0, 0)
    out_suf, lse_suf = attend_suffix(suffix_lengths, q_units, suffix_keys, suffix_values)
    part = attend(task_ids, page_table[:, 0], q_all, pieces, prefix_keys[0, 0], prefix_values[0, 0])
    parts = lax.all_to_all(part, "dev", 0, 0)
    merged = merge(parts, out_suf, lse_suf)
    return merged.reshape(KVH, OWN, QPK, HD).transpose(1, 0, 2, 3).reshape(OWN, KVH * QPK * HD)


def solution(mesh):
    placed = (
        P(("grp", "dev"), None),
        P(("grp", "dev"), None),
        P(("grp", "dev"), None),
        P("grp", "dev", None, None, None),
        P("grp", "dev", None, None, None),
        P(None, "dev", None),
        P("grp"),
        P(("grp", "dev"), None, None),
        P(("grp", "dev"), None, None),
        P(("grp", "dev")),
    )
    return jax.shard_map(
        per_device, mesh=mesh, in_specs=placed, out_specs=P(("grp", "dev"), None), check_vma=False
    )
```

```python
import functools

import jax
import jax.numpy as jnp
from jax import lax
from jax.experimental import pallas as pl
from jax.experimental.pallas import tpu as pltpu
from jax.sharding import PartitionSpec as P

HD = 128
KVH = 8
QPK = 8
MEMBERS = 16
OWN = 4
UNIT = OWN * QPK
SUF = 128
PPD = 4
PAGE = 64
SCALE = HD ** (-0.5)
LOG2E = 1.4426950408889634
ROWS_ALL = MEMBERS * UNIT
VMEM_LIMIT = 16 * 1024 * 1024
ATTEND_VMEM = 60 * 1024 * 1024
PARTS = (2, 3, 3)
STEPS = 2


def grp_index(x, y_hi, core):
    return (x % 4) * 4 + (y_hi % 2) * 2 + core


def grp_pairs(target):
    return [
        (grp_index(x, y, c), grp_index(*target(x, y, c)))
        for x in range(4)
        for y in range(2)
        for c in range(2)
    ]


def to_other_core(array):
    return lax.ppermute(array, "grp", grp_pairs(lambda x, y, c: (x, y, 1 - c)))


def along_y(array):
    return lax.ppermute(array, "grp", grp_pairs(lambda x, y, c: (x, 1 - y, c)))


def along_x(array):
    return lax.ppermute(array, "grp", grp_pairs(lambda x, y, c: (x + 1 - 2 * c, y, c)))


def after(array, *others):
    return lax.optimization_barrier((array, *others))[0]


def gather_root(own):
    other = to_other_core(own)
    near = along_x(own)
    across = along_y(own)
    near_other = along_x(other)
    far = along_x(near)
    across = after(across, near, near_other)
    across_near = along_x(across)
    across_other = to_other_core(across)
    across_near_other = along_x(across_other)
    across_far = along_x(across_near)
    received = [near, near_other, far, across_near, across_near_other, across_far]
    return [own, other, across, across_other] + received + [to_other_core(r) for r in received]


def nt_dot(a, b):
    return lax.dot_general(a, b, (((1,), (1,)), ((), ())), preferred_element_type=jnp.float32)


def split_three(value):
    first = value.astype(jnp.bfloat16)
    rest = value - first.astype(jnp.float32)
    second = rest.astype(jnp.bfloat16)
    third = (rest - second.astype(jnp.float32)).astype(jnp.bfloat16)
    return first, second, third


def flash_step(q, keys, values, state):
    scores = nt_dot(q, keys)
    peaks = jnp.max(scores, axis=1, keepdims=True)
    if state is not None:
        peaks = jnp.maximum(peaks, state[0])
    weights = jnp.exp2((scores - peaks) * (SCALE * LOG2E)).astype(jnp.bfloat16)
    widened = jnp.concatenate([values, jnp.ones_like(values)], axis=1)
    both = jnp.dot(weights, widened, preferred_element_type=jnp.float32)
    weighted, totals = both[:, :HD], both[:, HD:]
    if state is not None:
        factor = jnp.exp2((state[0] - peaks) * (SCALE * LOG2E))
        totals = totals + state[1] * factor
        weighted = weighted + state[2] * factor
    return peaks, totals, weighted


def attention_kernel(pieces, *refs):
    task_ref, table_ref, q_ref = refs[:3]
    piece_refs = refs[3 : 3 + pieces]
    pool_k, pool_v, out_ref, held_ref, peaks_ref, totals_ref, sems = refs[3 + pieces :]
    task = task_ref[0]
    root_rows = 128 * pieces
    copies = []
    first_head = 0
    for part, heads in enumerate(PARTS):
        lanes = pl.ds(first_head * HD, heads * HD)
        first_head += heads
        group = []
        for i, piece in enumerate(piece_refs):
            target = held_ref.at[:, pl.ds(i * 128, 128), lanes]
            group.append(pltpu.make_async_copy(piece.at[:, :, lanes], target, sems.at[part, i]))
        for j in range(PPD):
            page = table_ref[task, j]
            rows = pl.ds(root_rows + j * PAGE, PAGE)
            for side, pool in enumerate((pool_k, pool_v)):
                target = held_ref.at[side, rows, lanes]
                sem = sems.at[part, pieces + 2 * j + side]
                group.append(pltpu.make_async_copy(pool.at[page, :, lanes], target, sem))
        copies.append(group)
    for group in copies[:2]:
        for copy in group:
            copy.start()
    peaks_ref[...] = jnp.zeros_like(peaks_ref)
    totals_ref[...] = jnp.ones_like(totals_ref)
    size = (root_rows + PPD * PAGE) // STEPS
    lane = lax.broadcasted_iota(jnp.int32, (ROWS_ALL, HD), 1)

    def one_head(k):
        lanes = slice(k * HD, (k + 1) * HD)
        q = q_ref[:, k].reshape(ROWS_ALL, HD)
        state = None
        for i in range(STEPS):
            rows = slice(i * size, (i + 1) * size)
            state = flash_step(q, held_ref[0, rows, lanes], held_ref[1, rows, lanes], state)
        peaks, totals, weighted = state
        out_ref[:, k * UNIT : (k + 1) * UNIT] = (
            (weighted / totals).astype(jnp.bfloat16).reshape(MEMBERS, UNIT, HD)
        )
        peaks_ref[...] = jnp.where(lane == k, peaks, peaks_ref[...])
        totals_ref[...] = jnp.where(lane == k, totals, totals_ref[...])

    first_head = 0
    for part, heads in enumerate(PARTS):
        for copy in copies[part]:
            copy.wait()
        for k in range(first_head, first_head + heads):
            one_head(k)
        first_head += heads
        if part + 2 < len(PARTS):
            for copy in copies[part + 2]:
                copy.start()
    first, second, third = split_three(peaks_ref[...] * SCALE + jnp.log(totals_ref[...]))
    packed = (
        first.astype(jnp.float32)
        + pltpu.roll(second.astype(jnp.float32), KVH, 1)
        + pltpu.roll(third.astype(jnp.float32), 2 * KVH, 1)
    )
    packed = packed.reshape(MEMBERS, 2, UNIT // 2, HD)
    upper = pltpu.roll(packed[:, 1].reshape(ROWS_ALL // 2, HD), HD // 2, 1)
    packed = packed[:, 0].reshape(ROWS_ALL // 2, HD) + upper
    out_ref[:, KVH * UNIT :] = packed.astype(jnp.bfloat16).reshape(MEMBERS, UNIT // 2, HD)


def attend(task, table, q_all, pieces, pool_k, pool_v):
    keys = 128 * len(pieces) + PPD * PAGE
    vmem = pl.BlockSpec(memory_space=pltpu.VMEM)
    smem = pl.BlockSpec(memory_space=pltpu.SMEM)
    hbm = pl.BlockSpec(memory_space=pl.ANY)
    return pl.pallas_call(
        functools.partial(attention_kernel, len(pieces)),
        out_shape=jax.ShapeDtypeStruct((MEMBERS, KVH * UNIT + UNIT // 2, HD), jnp.bfloat16),
        in_specs=[smem, smem, vmem] + [hbm] * len(pieces) + [hbm, hbm],
        out_specs=vmem,
        scratch_shapes=[
            pltpu.VMEM((2, keys, KVH * HD), jnp.bfloat16),
            pltpu.VMEM((ROWS_ALL, HD), jnp.float32),
            pltpu.VMEM((ROWS_ALL, HD), jnp.float32),
            pltpu.SemaphoreType.DMA((len(PARTS), len(pieces) + 2 * PPD)),
        ],
        compiler_params=pltpu.CompilerParams(vmem_limit_bytes=ATTEND_VMEM),
        cost_estimate=attend_cost(keys),
        name="attend",
    )(task, table, q_all, *pieces, pool_k, pool_v)


def attend_cost(keys):
    return pl.CostEstimate(
        flops=8 * KVH * ROWS_ALL * keys * HD,
        bytes_accessed=4 * keys * KVH * HD,
        transcendentals=KVH * ROWS_ALL * keys,
    )


def suffix_kernel(length_ref, q_ref, k_ref, v_ref, out_ref, lse_ref):
    slots = OWN * SUF
    row = lax.broadcasted_iota(jnp.int32, (UNIT, slots), 0) % OWN
    slot = lax.broadcasted_iota(jnp.int32, (UNIT, slots), 1)
    live = jnp.zeros((UNIT, slots), jnp.bool_)
    for i in range(OWN):
        low = i * SUF
        live = live | ((row == i) & (slot >= low) & (slot < low + length_ref[i]))
    for k in range(KVH):
        lanes = slice(k * HD, (k + 1) * HD)
        keys = jnp.concatenate([k_ref[i, :, lanes] for i in range(OWN)], axis=0)
        values = jnp.concatenate([v_ref[i, :, lanes] for i in range(OWN)], axis=0)
        scores = jnp.where(live, nt_dot(q_ref[k], keys) * SCALE, -1e30)
        peaks = jnp.max(scores, axis=1, keepdims=True)
        weights = jnp.where(live, jnp.exp(scores - peaks), 0.0)
        totals = jnp.sum(weights, axis=1, keepdims=True)
        weighted = jnp.dot(weights.astype(jnp.bfloat16), values, preferred_element_type=jnp.float32)
        out_ref[k] = weighted / totals
        lse_ref[k] = jnp.broadcast_to(peaks + jnp.log(totals), (UNIT, HD))


def attend_suffix(lengths, q_units, suffix_keys, suffix_values):
    vmem = pl.BlockSpec(memory_space=pltpu.VMEM)
    shape = jax.ShapeDtypeStruct((KVH, UNIT, HD), jnp.float32)
    return pl.pallas_call(
        suffix_kernel,
        out_shape=(shape, shape),
        in_specs=[pl.BlockSpec(memory_space=pltpu.SMEM), vmem, vmem, vmem],
        out_specs=(vmem, vmem),
        compiler_params=pltpu.CompilerParams(vmem_limit_bytes=VMEM_LIMIT),
        cost_estimate=pl.CostEstimate(
            flops=4 * KVH * UNIT * OWN * SUF * HD, bytes_accessed=2 << 20, transcendentals=KVH * UNIT * OWN * SUF
        ),
        name="attend_suffix",
    )(lengths, q_units, suffix_keys, suffix_values)


def merge_kernel(parts_ref, out_suf_ref, lse_suf_ref, out_ref):
    stats = parts_ref[:, KVH * UNIT :].astype(jnp.float32)
    upper = pltpu.roll(stats.reshape(ROWS_ALL // 2, HD), HD // 2, 1).reshape(MEMBERS, UNIT // 2, HD)
    stats = jnp.concatenate([stats, upper], axis=1).reshape(ROWS_ALL, HD)
    lse = stats + pltpu.roll(stats, HD - KVH, 1) + pltpu.roll(stats, HD - 2 * KVH, 1)
    for k in range(KVH):
        own_lse = lse_suf_ref[k]
        column = jnp.broadcast_to(lse[:, k : k + 1], (ROWS_ALL, HD)).reshape(MEMBERS, UNIT, HD)
        top = jnp.maximum(jnp.max(column, axis=0), own_lse)
        factor = jnp.exp(column - top[None])
        own_factor = jnp.exp(own_lse - top)
        part = parts_ref[:, k * UNIT : (k + 1) * UNIT].astype(jnp.float32)
        weighted = jnp.sum(part * factor, axis=0) + out_suf_ref[k] * own_factor
        totals = jnp.sum(factor, axis=0) + own_factor
        result = (weighted / totals).astype(jnp.bfloat16)
        for g in range(QPK):
            head = k * QPK + g
            out_ref[:, head * HD : (head + 1) * HD] = result[g * OWN : (g + 1) * OWN]


def merge(parts, out_suf, lse_suf):
    vmem = pl.BlockSpec(memory_space=pltpu.VMEM)
    return pl.pallas_call(
        merge_kernel,
        out_shape=jax.ShapeDtypeStruct((OWN, KVH * QPK * HD), jnp.bfloat16),
        in_specs=[vmem] * 3,
        out_specs=vmem,
        compiler_params=pltpu.CompilerParams(vmem_limit_bytes=VMEM_LIMIT),
        cost_estimate=pl.CostEstimate(
            flops=4 * KVH * ROWS_ALL * HD, bytes_accessed=2 * KVH * ROWS_ALL * HD, transcendentals=0
        ),
        name="merge",
    )(parts, out_suf, lse_suf)


def per_device(
    queries,
    root_keys,
    root_values,
    prefix_keys,
    prefix_values,
    page_table,
    task_ids,
    suffix_keys,
    suffix_values,
    suffix_lengths,
):
    q_units = queries.reshape(OWN, KVH, QPK, HD).transpose(1, 2, 0, 3).reshape(KVH, UNIT, HD)
    pieces = gather_root(jnp.stack((root_keys, root_values)))
    q_tiled = jnp.broadcast_to(q_units[None], (MEMBERS, KVH, UNIT, HD))
    q_all = lax.all_to_all(q_tiled, "dev", 0, 0)
    out_suf, lse_suf = attend_suffix(suffix_lengths, q_units, suffix_keys, suffix_values)
    part = attend(task_ids, page_table[:, 0], q_all, pieces, prefix_keys[0, 0], prefix_values[0, 0])
    parts = lax.all_to_all(part, "dev", 0, 0)
    return merge(parts, out_suf, lse_suf)


def solution(mesh):
    placed = (
        P(("grp", "dev"), None),
        P(("grp", "dev"), None),
        P(("grp", "dev"), None),
        P("grp", "dev", None, None, None),
        P("grp", "dev", None, None, None),
        P(None, "dev", None),
        P("grp"),
        P(("grp", "dev"), None, None),
        P(("grp", "dev"), None, None),
        P(("grp", "dev")),
    )
    return jax.shard_map(
        per_device, mesh=mesh, in_specs=placed, out_specs=P(("grp", "dev"), None), check_vma=False
    )
```

```python
import functools

import jax
import jax.numpy as jnp
from jax import lax
from jax.experimental import pallas as pl
from jax.experimental.pallas import tpu as pltpu
from jax.sharding import PartitionSpec as P

HD = 128
KVH = 8
QPK = 8
MEMBERS = 16
OWN = 4
UNIT = OWN * QPK
SUF = 128
PPD = 4
PAGE = 64
SCALE = HD ** (-0.5)
LOG2E = 1.4426950408889634
ROWS_ALL = MEMBERS * UNIT
VMEM_LIMIT = 16 * 1024 * 1024
ATTEND_VMEM = 60 * 1024 * 1024
PARTS = (2, 3, 3)
STEPS = 1


def grp_index(x, y_hi, core):
    return (x % 4) * 4 + (y_hi % 2) * 2 + core


def grp_pairs(target):
    return [
        (grp_index(x, y, c), grp_index(*target(x, y, c)))
        for x in range(4)
        for y in range(2)
        for c in range(2)
    ]


def to_other_core(array):
    return lax.ppermute(array, "grp", grp_pairs(lambda x, y, c: (x, y, 1 - c)))


def along_y(array):
    return lax.ppermute(array, "grp", grp_pairs(lambda x, y, c: (x, 1 - y, c)))


def along_x(array):
    return lax.ppermute(array, "grp", grp_pairs(lambda x, y, c: (x + 1 - 2 * c, y, c)))


def after(array, *others):
    return lax.optimization_barrier((array, *others))[0]


def gather_root(own):
    other = to_other_core(own)
    near = along_x(own)
    across = along_y(own)
    near_other = along_x(other)
    far = along_x(near)
    across = after(across, near, near_other)
    across_near = along_x(across)
    across_other = to_other_core(across)
    across_near_other = along_x(across_other)
    across_far = along_x(across_near)
    received = [near, near_other, far, across_near, across_near_other, across_far]
    return [own, other, across, across_other] + received + [to_other_core(r) for r in received]


def nt_dot(a, b):
    return lax.dot_general(a, b, (((1,), (1,)), ((), ())), preferred_element_type=jnp.float32)


def split_three(value):
    first = value.astype(jnp.bfloat16)
    rest = value - first.astype(jnp.float32)
    second = rest.astype(jnp.bfloat16)
    third = (rest - second.astype(jnp.float32)).astype(jnp.bfloat16)
    return first, second, third


def flash_step(scores, values, state):
    peaks = jnp.max(scores, axis=1, keepdims=True)
    if state is not None:
        peaks = jnp.maximum(peaks, state[0])
    weights = jnp.exp2((scores - peaks) * (SCALE * LOG2E)).astype(jnp.bfloat16)
    widened = jnp.concatenate([values, jnp.ones_like(values)], axis=1)
    both = jnp.dot(weights, widened, preferred_element_type=jnp.float32)
    weighted, totals = both[:, :HD], both[:, HD:]
    if state is not None:
        factor = jnp.exp2((state[0] - peaks) * (SCALE * LOG2E))
        totals = totals + state[1] * factor
        weighted = weighted + state[2] * factor
    return peaks, totals, weighted


def attention_kernel(pieces, *refs):
    task_ref, table_ref, q_ref = refs[:3]
    piece_refs = refs[3 : 3 + pieces]
    pool_k, pool_v, out_ref, held_ref, peaks_ref, totals_ref, sems = refs[3 + pieces :]
    task = task_ref[0]
    root_rows = 128 * pieces
    copies = []
    first_head = 0
    for part, heads in enumerate(PARTS):
        lanes = pl.ds(first_head * HD, heads * HD)
        first_head += heads
        group = []
        for i, piece in enumerate(piece_refs):
            target = held_ref.at[:, pl.ds(i * 128, 128), lanes]
            group.append(pltpu.make_async_copy(piece.at[:, :, lanes], target, sems.at[part, i]))
        for j in range(PPD):
            page = table_ref[task, j]
            rows = pl.ds(root_rows + j * PAGE, PAGE)
            for side, pool in enumerate((pool_k, pool_v)):
                target = held_ref.at[side, rows, lanes]
                sem = sems.at[part, pieces + 2 * j + side]
                group.append(pltpu.make_async_copy(pool.at[page, :, lanes], target, sem))
        copies.append(group)
    for group in copies[:2]:
        for copy in group:
            copy.start()
    peaks_ref[...] = jnp.zeros_like(peaks_ref)
    totals_ref[...] = jnp.ones_like(totals_ref)
    size = (root_rows + PPD * PAGE) // STEPS
    lane = lax.broadcasted_iota(jnp.int32, (ROWS_ALL, HD), 1)

    def scores_of(k, i):
        keys = held_ref[0, i * size : (i + 1) * size, k * HD : (k + 1) * HD]
        return nt_dot(q_ref[:, k].reshape(ROWS_ALL, HD), keys)

    def finish_head(k, state):
        peaks, totals, weighted = state
        out_ref[:, k * UNIT : (k + 1) * UNIT] = (
            (weighted / totals).astype(jnp.bfloat16).reshape(MEMBERS, UNIT, HD)
        )
        peaks_ref[...] = jnp.where(lane == k, peaks, peaks_ref[...])
        totals_ref[...] = jnp.where(lane == k, totals, totals_ref[...])

    first_head = 0
    for part, heads in enumerate(PARTS):
        for copy in copies[part]:
            copy.wait()
        steps = [(k, i) for k in range(first_head, first_head + heads) for i in range(STEPS)]
        first_head += heads
        scores = scores_of(*steps[0])
        state = None
        for (k, i), later in zip(steps, steps[1:] + [None]):
            later_scores = None if later is None else scores_of(*later)
            values = held_ref[1, i * size : (i + 1) * size, k * HD : (k + 1) * HD]
            state = flash_step(scores, values, state)
            scores = later_scores
            if i == STEPS - 1:
                finish_head(k, state)
                state = None
        if part + 2 < len(PARTS):
            for copy in copies[part + 2]:
                copy.start()
    first, second, third = split_three(peaks_ref[...] * SCALE + jnp.log(totals_ref[...]))
    packed = (
        first.astype(jnp.float32)
        + pltpu.roll(second.astype(jnp.float32), KVH, 1)
        + pltpu.roll(third.astype(jnp.float32), 2 * KVH, 1)
    )
    packed = packed.reshape(MEMBERS, 2, UNIT // 2, HD)
    upper = pltpu.roll(packed[:, 1].reshape(ROWS_ALL // 2, HD), HD // 2, 1)
    packed = packed[:, 0].reshape(ROWS_ALL // 2, HD) + upper
    out_ref[:, KVH * UNIT :] = packed.astype(jnp.bfloat16).reshape(MEMBERS, UNIT // 2, HD)


def attend(task, table, q_all, pieces, pool_k, pool_v):
    keys = 128 * len(pieces) + PPD * PAGE
    vmem = pl.BlockSpec(memory_space=pltpu.VMEM)
    smem = pl.BlockSpec(memory_space=pltpu.SMEM)
    hbm = pl.BlockSpec(memory_space=pl.ANY)
    return pl.pallas_call(
        functools.partial(attention_kernel, len(pieces)),
        out_shape=jax.ShapeDtypeStruct((MEMBERS, KVH * UNIT + UNIT // 2, HD), jnp.bfloat16),
        in_specs=[smem, smem, vmem] + [hbm] * len(pieces) + [hbm, hbm],
        out_specs=vmem,
        scratch_shapes=[
            pltpu.VMEM((2, keys, KVH * HD), jnp.bfloat16),
            pltpu.VMEM((ROWS_ALL, HD), jnp.float32),
            pltpu.VMEM((ROWS_ALL, HD), jnp.float32),
            pltpu.SemaphoreType.DMA((len(PARTS), len(pieces) + 2 * PPD)),
        ],
        compiler_params=pltpu.CompilerParams(vmem_limit_bytes=ATTEND_VMEM),
        cost_estimate=attend_cost(keys),
        name="attend",
    )(task, table, q_all, *pieces, pool_k, pool_v)


def attend_cost(keys):
    return pl.CostEstimate(
        flops=8 * KVH * ROWS_ALL * keys * HD,
        bytes_accessed=4 * keys * KVH * HD,
        transcendentals=KVH * ROWS_ALL * keys,
    )


def spread_kernel(q_ref, out_ref, sems):
    copies = [pltpu.make_async_copy(q_ref, out_ref.at[m], sems.at[m]) for m in range(MEMBERS)]
    for copy in copies:
        copy.start()
    for copy in copies:
        copy.wait()


def spread(q_units):
    return pl.pallas_call(
        spread_kernel,
        out_shape=jax.ShapeDtypeStruct((MEMBERS, KVH, UNIT, HD), jnp.bfloat16),
        in_specs=[pl.BlockSpec(memory_space=pltpu.VMEM)],
        out_specs=pl.BlockSpec(memory_space=pl.ANY),
        scratch_shapes=[pltpu.SemaphoreType.DMA((MEMBERS,))],
        compiler_params=pltpu.CompilerParams(vmem_limit_bytes=VMEM_LIMIT),
        cost_estimate=pl.CostEstimate(flops=0, bytes_accessed=MEMBERS * KVH * UNIT * HD * 2, transcendentals=0),
        name="spread",
    )(q_units)


def suffix_kernel(length_ref, q_ref, k_ref, v_ref, out_ref, lse_ref):
    slots = OWN * SUF
    row = lax.broadcasted_iota(jnp.int32, (UNIT, slots), 0) % OWN
    slot = lax.broadcasted_iota(jnp.int32, (UNIT, slots), 1)
    live = jnp.zeros((UNIT, slots), jnp.bool_)
    for i in range(OWN):
        low = i * SUF
        live = live | ((row == i) & (slot >= low) & (slot < low + length_ref[i]))
    for k in range(KVH):
        lanes = slice(k * HD, (k + 1) * HD)
        keys = jnp.concatenate([k_ref[i, :, lanes] for i in range(OWN)], axis=0)
        values = jnp.concatenate([v_ref[i, :, lanes] for i in range(OWN)], axis=0)
        scores = jnp.where(live, nt_dot(q_ref[k], keys) * SCALE, -1e30)
        peaks = jnp.max(scores, axis=1, keepdims=True)
        weights = jnp.where(live, jnp.exp(scores - peaks), 0.0)
        totals = jnp.sum(weights, axis=1, keepdims=True)
        weighted = jnp.dot(weights.astype(jnp.bfloat16), values, preferred_element_type=jnp.float32)
        out_ref[k] = weighted / totals
        lse_ref[k] = jnp.broadcast_to(peaks + jnp.log(totals), (UNIT, HD))


def attend_suffix(lengths, q_units, suffix_keys, suffix_values):
    vmem = pl.BlockSpec(memory_space=pltpu.VMEM)
    shape = jax.ShapeDtypeStruct((KVH, UNIT, HD), jnp.float32)
    return pl.pallas_call(
        suffix_kernel,
        out_shape=(shape, shape),
        in_specs=[pl.BlockSpec(memory_space=pltpu.SMEM), vmem, vmem, vmem],
        out_specs=(vmem, vmem),
        compiler_params=pltpu.CompilerParams(vmem_limit_bytes=VMEM_LIMIT),
        cost_estimate=pl.CostEstimate(
            flops=4 * KVH * UNIT * OWN * SUF * HD, bytes_accessed=2 << 20, transcendentals=KVH * UNIT * OWN * SUF
        ),
        name="attend_suffix",
    )(lengths, q_units, suffix_keys, suffix_values)


def merge_kernel(parts_ref, out_suf_ref, lse_suf_ref, out_ref):
    stats = parts_ref[:, KVH * UNIT :].astype(jnp.float32)
    upper = pltpu.roll(stats.reshape(ROWS_ALL // 2, HD), HD // 2, 1).reshape(MEMBERS, UNIT // 2, HD)
    stats = jnp.concatenate([stats, upper], axis=1).reshape(ROWS_ALL, HD)
    lse = stats + pltpu.roll(stats, HD - KVH, 1) + pltpu.roll(stats, HD - 2 * KVH, 1)
    for k in range(KVH):
        own_lse = lse_suf_ref[k]
        column = jnp.broadcast_to(lse[:, k : k + 1], (ROWS_ALL, HD)).reshape(MEMBERS, UNIT, HD)
        top = jnp.maximum(jnp.max(column, axis=0), own_lse)
        factor = jnp.exp(column - top[None])
        own_factor = jnp.exp(own_lse - top)
        part = parts_ref[:, k * UNIT : (k + 1) * UNIT].astype(jnp.float32)
        weighted = jnp.sum(part * factor, axis=0) + out_suf_ref[k] * own_factor
        totals = jnp.sum(factor, axis=0) + own_factor
        result = (weighted / totals).astype(jnp.bfloat16)
        for g in range(QPK):
            head = k * QPK + g
            out_ref[:, head * HD : (head + 1) * HD] = result[g * OWN : (g + 1) * OWN]


def merge(parts, out_suf, lse_suf):
    vmem = pl.BlockSpec(memory_space=pltpu.VMEM)
    return pl.pallas_call(
        merge_kernel,
        out_shape=jax.ShapeDtypeStruct((OWN, KVH * QPK * HD), jnp.bfloat16),
        in_specs=[vmem] * 3,
        out_specs=vmem,
        compiler_params=pltpu.CompilerParams(vmem_limit_bytes=VMEM_LIMIT),
        cost_estimate=pl.CostEstimate(
            flops=4 * KVH * ROWS_ALL * HD, bytes_accessed=2 * KVH * ROWS_ALL * HD, transcendentals=0
        ),
        name="merge",
    )(parts, out_suf, lse_suf)


def per_device(
    queries,
    root_keys,
    root_values,
    prefix_keys,
    prefix_values,
    page_table,
    task_ids,
    suffix_keys,
    suffix_values,
    suffix_lengths,
):
    q_units = queries.reshape(OWN, KVH, QPK, HD).transpose(1, 2, 0, 3).reshape(KVH, UNIT, HD)
    pieces = gather_root(jnp.stack((root_keys, root_values)))
    q_all = lax.all_to_all(spread(q_units), "dev", 0, 0)
    out_suf, lse_suf = attend_suffix(suffix_lengths, q_units, suffix_keys, suffix_values)
    part = attend(task_ids, page_table[:, 0], q_all, pieces, prefix_keys[0, 0], prefix_values[0, 0])
    parts = lax.all_to_all(part, "dev", 0, 0)
    return merge(parts, out_suf, lse_suf)


def solution(mesh):
    placed = (
        P(("grp", "dev"), None),
        P(("grp", "dev"), None),
        P(("grp", "dev"), None),
        P("grp", "dev", None, None, None),
        P("grp", "dev", None, None, None),
        P(None, "dev", None),
        P("grp"),
        P(("grp", "dev"), None, None),
        P(("grp", "dev"), None, None),
        P(("grp", "dev")),
    )
    return jax.shard_map(
        per_device, mesh=mesh, in_specs=placed, out_specs=P(("grp", "dev"), None), check_vma=False
    )
```

```python
import functools

import jax
import jax.numpy as jnp
from jax import lax
from jax.experimental import pallas as pl
from jax.experimental.pallas import tpu as pltpu
from jax.sharding import PartitionSpec as P

HD = 128
KVH = 8
QPK = 8
MEMBERS = 16
OWN = 4
UNIT = OWN * QPK
SUF = 128
PPD = 4
PAGE = 64
SCALE = HD ** (-0.5)
LOG2E = 1.4426950408889634
ROWS_ALL = MEMBERS * UNIT
VMEM_LIMIT = 16 * 1024 * 1024
ATTEND_VMEM = 60 * 1024 * 1024
PARTS = (2, 3, 3)
STEPS = 1


def grp_index(x, y_hi, core):
    return (x % 4) * 4 + (y_hi % 2) * 2 + core


def grp_pairs(target):
    return [
        (grp_index(x, y, c), grp_index(*target(x, y, c)))
        for x in range(4)
        for y in range(2)
        for c in range(2)
    ]


def to_other_core(array):
    return lax.ppermute(array, "grp", grp_pairs(lambda x, y, c: (x, y, 1 - c)))


def along_y(array):
    return lax.ppermute(array, "grp", grp_pairs(lambda x, y, c: (x, 1 - y, c)))


def along_x(array):
    return lax.ppermute(array, "grp", grp_pairs(lambda x, y, c: (x + 1 - 2 * c, y, c)))


def after(array, *others):
    return lax.optimization_barrier((array, *others))[0]


def gather_root(own):
    other = to_other_core(own)
    near = along_x(own)
    across = along_y(own)
    near_other = along_x(other)
    far = along_x(near)
    across = after(across, near, near_other)
    across_near = along_x(across)
    across_other = to_other_core(across)
    across_near_other = along_x(after(across_other, far))
    across_far = along_x(across_near)
    received = [near, near_other, far, across_near, across_near_other, across_far]
    return [own, other, across, across_other] + received + [to_other_core(r) for r in received]


def nt_dot(a, b):
    return lax.dot_general(a, b, (((1,), (1,)), ((), ())), preferred_element_type=jnp.float32)


def split_three(value):
    first = value.astype(jnp.bfloat16)
    rest = value - first.astype(jnp.float32)
    second = rest.astype(jnp.bfloat16)
    third = (rest - second.astype(jnp.float32)).astype(jnp.bfloat16)
    return first, second, third


def flash_step(scores, values, state):
    peaks = jnp.max(scores, axis=1, keepdims=True)
    if state is not None:
        peaks = jnp.maximum(peaks, state[0])
    weights = jnp.exp2((scores - peaks) * (SCALE * LOG2E)).astype(jnp.bfloat16)
    widened = jnp.concatenate([values, jnp.ones_like(values)], axis=1)
    both = jnp.dot(weights, widened, preferred_element_type=jnp.float32)
    weighted, totals = both[:, :HD], both[:, HD:]
    if state is not None:
        factor = jnp.exp2((state[0] - peaks) * (SCALE * LOG2E))
        totals = totals + state[1] * factor
        weighted = weighted + state[2] * factor
    return peaks, totals, weighted


def attention_kernel(pieces, *refs):
    task_ref, table_ref, q_ref = refs[:3]
    piece_refs = refs[3 : 3 + pieces]
    pool_k, pool_v, out_ref, held_ref, peaks_ref, totals_ref, sems = refs[3 + pieces :]
    task = task_ref[0]
    root_rows = 128 * pieces
    copies = []
    first_head = 0
    for part, heads in enumerate(PARTS):
        lanes = pl.ds(first_head * HD, heads * HD)
        first_head += heads
        group = []
        for i, piece in enumerate(piece_refs):
            target = held_ref.at[:, pl.ds(i * 128, 128), lanes]
            group.append(pltpu.make_async_copy(piece.at[:, :, lanes], target, sems.at[part, i]))
        for j in range(PPD):
            page = table_ref[task, j]
            rows = pl.ds(root_rows + j * PAGE, PAGE)
            for side, pool in enumerate((pool_k, pool_v)):
                target = held_ref.at[side, rows, lanes]
                sem = sems.at[part, pieces + 2 * j + side]
                group.append(pltpu.make_async_copy(pool.at[page, :, lanes], target, sem))
        copies.append(group)
    for group in copies[:2]:
        for copy in group:
            copy.start()
    peaks_ref[...] = jnp.zeros_like(peaks_ref)
    totals_ref[...] = jnp.ones_like(totals_ref)
    size = (root_rows + PPD * PAGE) // STEPS
    lane = lax.broadcasted_iota(jnp.int32, (ROWS_ALL, HD), 1)

    def scores_of(k, i):
        keys = held_ref[0, i * size : (i + 1) * size, k * HD : (k + 1) * HD]
        return nt_dot(q_ref[:, k].reshape(ROWS_ALL, HD), keys)

    def finish_head(k, state):
        peaks, totals, weighted = state
        out_ref[:, k * UNIT : (k + 1) * UNIT] = (
            (weighted / totals).astype(jnp.bfloat16).reshape(MEMBERS, UNIT, HD)
        )
        peaks_ref[...] = jnp.where(lane == k, peaks, peaks_ref[...])
        totals_ref[...] = jnp.where(lane == k, totals, totals_ref[...])

    first_head = 0
    for part, heads in enumerate(PARTS):
        for copy in copies[part]:
            copy.wait()
        steps = [(k, i) for k in range(first_head, first_head + heads) for i in range(STEPS)]
        first_head += heads
        scores = scores_of(*steps[0])
        state = None
        for (k, i), later in zip(steps, steps[1:] + [None]):
            later_scores = None if later is None else scores_of(*later)
            values = held_ref[1, i * size : (i + 1) * size, k * HD : (k + 1) * HD]
            state = flash_step(scores, values, state)
            scores = later_scores
            if i == STEPS - 1:
                finish_head(k, state)
                state = None
        if part + 2 < len(PARTS):
            for copy in copies[part + 2]:
                copy.start()
    first, second, third = split_three(peaks_ref[...] * SCALE + jnp.log(totals_ref[...]))
    packed = (
        first.astype(jnp.float32)
        + pltpu.roll(second.astype(jnp.float32), KVH, 1)
        + pltpu.roll(third.astype(jnp.float32), 2 * KVH, 1)
    )
    packed = packed.reshape(MEMBERS, 2, UNIT // 2, HD)
    upper = pltpu.roll(packed[:, 1].reshape(ROWS_ALL // 2, HD), HD // 2, 1)
    packed = packed[:, 0].reshape(ROWS_ALL // 2, HD) + upper
    out_ref[:, KVH * UNIT :] = packed.astype(jnp.bfloat16).reshape(MEMBERS, UNIT // 2, HD)


def attend(task, table, q_all, pieces, pool_k, pool_v):
    keys = 128 * len(pieces) + PPD * PAGE
    vmem = pl.BlockSpec(memory_space=pltpu.VMEM)
    smem = pl.BlockSpec(memory_space=pltpu.SMEM)
    hbm = pl.BlockSpec(memory_space=pl.ANY)
    return pl.pallas_call(
        functools.partial(attention_kernel, len(pieces)),
        out_shape=jax.ShapeDtypeStruct((MEMBERS, KVH * UNIT + UNIT // 2, HD), jnp.bfloat16),
        in_specs=[smem, smem, vmem] + [hbm] * len(pieces) + [hbm, hbm],
        out_specs=vmem,
        scratch_shapes=[
            pltpu.VMEM((2, keys, KVH * HD), jnp.bfloat16),
            pltpu.VMEM((ROWS_ALL, HD), jnp.float32),
            pltpu.VMEM((ROWS_ALL, HD), jnp.float32),
            pltpu.SemaphoreType.DMA((len(PARTS), len(pieces) + 2 * PPD)),
        ],
        compiler_params=pltpu.CompilerParams(vmem_limit_bytes=ATTEND_VMEM),
        cost_estimate=attend_cost(keys),
        name="attend",
    )(task, table, q_all, *pieces, pool_k, pool_v)


def attend_cost(keys):
    return pl.CostEstimate(
        flops=8 * KVH * ROWS_ALL * keys * HD,
        bytes_accessed=4 * keys * KVH * HD,
        transcendentals=KVH * ROWS_ALL * keys,
    )


def spread_kernel(q_ref, out_ref, sems):
    copies = [pltpu.make_async_copy(q_ref, out_ref.at[m], sems.at[m]) for m in range(MEMBERS)]
    for copy in copies:
        copy.start()
    for copy in copies:
        copy.wait()


def spread(q_units):
    return pl.pallas_call(
        spread_kernel,
        out_shape=jax.ShapeDtypeStruct((MEMBERS, KVH, UNIT, HD), jnp.bfloat16),
        in_specs=[pl.BlockSpec(memory_space=pltpu.VMEM)],
        out_specs=pl.BlockSpec(memory_space=pl.ANY),
        scratch_shapes=[pltpu.SemaphoreType.DMA((MEMBERS,))],
        compiler_params=pltpu.CompilerParams(vmem_limit_bytes=VMEM_LIMIT),
        cost_estimate=pl.CostEstimate(flops=0, bytes_accessed=MEMBERS * KVH * UNIT * HD * 2, transcendentals=0),
        name="spread",
    )(q_units)


def suffix_kernel(length_ref, q_ref, k_ref, v_ref, out_ref, lse_ref):
    slots = OWN * SUF
    row = lax.broadcasted_iota(jnp.int32, (UNIT, slots), 0) % OWN
    slot = lax.broadcasted_iota(jnp.int32, (UNIT, slots), 1)
    live = jnp.zeros((UNIT, slots), jnp.bool_)
    for i in range(OWN):
        low = i * SUF
        live = live | ((row == i) & (slot >= low) & (slot < low + length_ref[i]))
    for k in range(KVH):
        lanes = slice(k * HD, (k + 1) * HD)
        keys = jnp.concatenate([k_ref[i, :, lanes] for i in range(OWN)], axis=0)
        values = jnp.concatenate([v_ref[i, :, lanes] for i in range(OWN)], axis=0)
        scores = jnp.where(live, nt_dot(q_ref[k], keys) * SCALE, -1e30)
        peaks = jnp.max(scores, axis=1, keepdims=True)
        weights = jnp.where(live, jnp.exp(scores - peaks), 0.0)
        totals = jnp.sum(weights, axis=1, keepdims=True)
        weighted = jnp.dot(weights.astype(jnp.bfloat16), values, preferred_element_type=jnp.float32)
        out_ref[k] = weighted / totals
        lse_ref[k] = jnp.broadcast_to(peaks + jnp.log(totals), (UNIT, HD))


def attend_suffix(lengths, q_units, suffix_keys, suffix_values):
    vmem = pl.BlockSpec(memory_space=pltpu.VMEM)
    shape = jax.ShapeDtypeStruct((KVH, UNIT, HD), jnp.float32)
    return pl.pallas_call(
        suffix_kernel,
        out_shape=(shape, shape),
        in_specs=[pl.BlockSpec(memory_space=pltpu.SMEM), vmem, vmem, vmem],
        out_specs=(vmem, vmem),
        compiler_params=pltpu.CompilerParams(vmem_limit_bytes=VMEM_LIMIT),
        cost_estimate=pl.CostEstimate(
            flops=4 * KVH * UNIT * OWN * SUF * HD, bytes_accessed=2 << 20, transcendentals=KVH * UNIT * OWN * SUF
        ),
        name="attend_suffix",
    )(lengths, q_units, suffix_keys, suffix_values)


def merge_kernel(parts_ref, out_suf_ref, lse_suf_ref, out_ref):
    stats = parts_ref[:, KVH * UNIT :].astype(jnp.float32)
    upper = pltpu.roll(stats.reshape(ROWS_ALL // 2, HD), HD // 2, 1).reshape(MEMBERS, UNIT // 2, HD)
    stats = jnp.concatenate([stats, upper], axis=1).reshape(ROWS_ALL, HD)
    lse = stats + pltpu.roll(stats, HD - KVH, 1) + pltpu.roll(stats, HD - 2 * KVH, 1)
    for k in range(KVH):
        own_lse = lse_suf_ref[k]
        column = jnp.broadcast_to(lse[:, k : k + 1], (ROWS_ALL, HD)).reshape(MEMBERS, UNIT, HD)
        top = jnp.maximum(jnp.max(column, axis=0), own_lse)
        factor = jnp.exp(column - top[None])
        own_factor = jnp.exp(own_lse - top)
        part = parts_ref[:, k * UNIT : (k + 1) * UNIT].astype(jnp.float32)
        weighted = jnp.sum(part * factor, axis=0) + out_suf_ref[k] * own_factor
        totals = jnp.sum(factor, axis=0) + own_factor
        result = (weighted / totals).astype(jnp.bfloat16)
        for g in range(QPK):
            head = k * QPK + g
            out_ref[:, head * HD : (head + 1) * HD] = result[g * OWN : (g + 1) * OWN]


def merge(parts, out_suf, lse_suf):
    vmem = pl.BlockSpec(memory_space=pltpu.VMEM)
    return pl.pallas_call(
        merge_kernel,
        out_shape=jax.ShapeDtypeStruct((OWN, KVH * QPK * HD), jnp.bfloat16),
        in_specs=[vmem] * 3,
        out_specs=vmem,
        compiler_params=pltpu.CompilerParams(vmem_limit_bytes=VMEM_LIMIT),
        cost_estimate=pl.CostEstimate(
            flops=4 * KVH * ROWS_ALL * HD, bytes_accessed=2 * KVH * ROWS_ALL * HD, transcendentals=0
        ),
        name="merge",
    )(parts, out_suf, lse_suf)


def per_device(
    queries,
    root_keys,
    root_values,
    prefix_keys,
    prefix_values,
    page_table,
    task_ids,
    suffix_keys,
    suffix_values,
    suffix_lengths,
):
    q_units = queries.reshape(OWN, KVH, QPK, HD).transpose(1, 2, 0, 3).reshape(KVH, UNIT, HD)
    pieces = gather_root(jnp.stack((root_keys, root_values)))
    q_all = lax.all_to_all(spread(q_units), "dev", 0, 0)
    out_suf, lse_suf = attend_suffix(suffix_lengths, q_units, suffix_keys, suffix_values)
    part = attend(task_ids, page_table[:, 0], q_all, pieces, prefix_keys[0, 0], prefix_values[0, 0])
    parts = lax.all_to_all(part, "dev", 0, 0)
    return merge(parts, out_suf, lse_suf)


def solution(mesh):
    placed = (
        P(("grp", "dev"), None),
        P(("grp", "dev"), None),
        P(("grp", "dev"), None),
        P("grp", "dev", None, None, None),
        P("grp", "dev", None, None, None),
        P(None, "dev", None),
        P("grp"),
        P(("grp", "dev"), None, None),
        P(("grp", "dev"), None, None),
        P(("grp", "dev")),
    )
    return jax.shard_map(
        per_device, mesh=mesh, in_specs=placed, out_specs=P(("grp", "dev"), None), check_vma=False
    )
```
